32 devices in a mesh: bond: 8 (over z, y), mpo: 4 (over x, core).
Axes of the slice: x: 2, y: 2, z: 4, core: 2. Of those that a mesh axis runs over, the one named last changes fastest.
Arguments:
- wave_blocks: bfloat16 [256, 8, 64, 256], P('bond'), may hold values from -6 to 6
- left_env: bfloat16 [256, 20, 4096], P('bond', 'mpo'), may hold values from -0.75 to 0.75
- right_env: bfloat16 [256, 20, 4096], P('bond', 'mpo'), may hold values from -0.75 to 0.75
- mpo_coef: float32 [20, 8], P('mpo'), may hold values from -3 to 3
- mpo_mask: int32 [20, 8], P('mpo'), may hold values 0 or 1
- right_sector: int32 [256, 8], replicated, may hold values from 0 to 255, as said below
Outputs:
- sigma_blocks: bfloat16 [256, 8, 64, 256], P('bond')
The draws below stay inside these ranges and needn't reach their ends.
Inputs may be any that keep to these rules, and one draw needn't show every extreme that they name: `right_sector`: right sector b is held by bond device b // 32. The 256 blocks of the left sectors of one bond device (rows in order) name sectors of at most 64 blocks on any one bond device, and exactly 64 on some.
All inputs are finite; a program needn't handle non-finite values. No bound on the sum of `mpo_mask` on one device may be relied on, other than what follows from the above.
Results may differ from the reference program's by a relative error of at most 0.013.
Values may be sent and summed in bfloat16 or wider, within the bound.
A program may use at most 512 MiB of HBM per device.

```python
import jax
import jax.numpy as jnp
from jax import lax

BLK = 64
NSEC = 256
NPB = 8
TERMS = 20
NVEC = 4
SEC_DEV = 32
NB_DEV = 256
CAP = 64
N_BOND = 8
N_MPO = 4


def draw_right_sector(key, part):
    key_list = jax.random.split(key, 5)
    slot_total = N_BOND * CAP
    slot_owner = jnp.arange(slot_total, dtype=jnp.int32) // CAP
    busy_level = jax.random.randint(key_list[0], (N_BOND,), 0, 4)
    favorite = jax.random.randint(key_list[1], (N_BOND,), 0, N_BOND)
    noise_part = jax.random.randint(key_list[2], (N_BOND, slot_total), 0, 4096)
    scores = noise_part + busy_level[slot_owner][None, :] * 4096
    scores = scores + (slot_owner[None, :] == favorite[:, None]).astype(jnp.int32) * 65536
    scores = scores * slot_total + jnp.arange(slot_total, dtype=jnp.int32)[None, :]
    chosen = lax.top_k(scores, NB_DEV)[1].astype(jnp.int32)
    shuffle_keys = jax.random.randint(key_list[3], (N_BOND, NB_DEV), 0, 1 << 20) * NB_DEV
    shuffle_keys = shuffle_keys + jnp.arange(NB_DEV, dtype=jnp.int32)[None, :]
    order_ids = jnp.argsort(shuffle_keys, axis=1)
    chosen = jnp.take_along_axis(chosen, order_ids, axis=1)
    local_ids = jax.random.randint(key_list[4], (N_BOND, NB_DEV), 0, SEC_DEV)
    return (chosen // CAP * SEC_DEV + local_ids).reshape(NSEC, NPB).astype(jnp.int32)


def plant(values, rng, smallest, top_value):
    spot = [jax.random.randint(jax.random.fold_in(rng, axis), (), 0, length) for axis, length in enumerate(values.shape)]
    main_axis = values.shape.index(max(values.shape))
    beside = spot[:main_axis] + [(spot[main_axis] + 1) % values.shape[main_axis]] + spot[main_axis + 1:]
    return values.at[tuple(spot)].set(smallest).at[tuple(beside)].set(top_value)


def shard_levels(rng, shape, cuts, low, high):
    loudness = 1.0
    for axis_at, parts in cuts:
        steps = jax.random.uniform(jax.random.fold_in(jax.random.fold_in(rng, 6), axis_at), (parts,), jnp.float32, low / len(cuts), high / len(cuts))
        loudness = loudness * jnp.repeat(jnp.exp(steps), shape[axis_at] // parts).reshape((-1,) + (1,) * (len(shape) - 1 - axis_at))
    return loudness


def normal_values(own_key, extent, width, limit, cuts=(), kind=jnp.bfloat16):
    values = jax.random.normal(own_key, extent, jnp.float32) * width
    if len(cuts) > 0:
        values = shard_levels(own_key, extent, cuts, -0.22, 0.18) * values
    return jnp.clip(values, min=-limit, max=limit).astype(kind)


def setup_inputs(seed: int = 0) -> dict:
    seeds = jax.random.split(jax.random.key(seed), 7)
    wave_blocks = normal_values(seeds[0], (NSEC, NPB, BLK, NVEC * BLK), 1.0, 6.0, ((0, 8),))
    left_env = normal_values(seeds[1], (NSEC, TERMS, BLK * BLK), BLK ** -0.5, 0.75, ((0, 8), (1, 4)))
    right_env = normal_values(seeds[2], (NSEC, TERMS, BLK * BLK), BLK ** -0.5, 0.75, ((0, 8), (1, 4)))
    mpo_coef = normal_values(seeds[3], (TERMS, NPB), 0.5, 3.0, ((0, 4),), jnp.float32)
    mpo_mask = plant((jax.random.randint(seeds[4], (TERMS, NPB), 0, 2) < 1).astype(jnp.int32), jax.random.fold_in(seeds[4], 1), 0, 1)
    right_sector = draw_right_sector(jax.random.fold_in(seeds[6], 71), 0)
    return {"wave_blocks": wave_blocks, "left_env": left_env, "right_env": right_env, "mpo_coef": mpo_coef, "mpo_mask": mpo_mask, "right_sector": right_sector}


def to_bfloat(values):
    return lax.optimization_barrier(values.astype(jnp.bfloat16)).astype(jnp.float32)


def reference(wave_blocks, left_env, right_env, mpo_coef, mpo_mask, right_sector):
    term_gains = mpo_coef * mpo_mask.astype(jnp.float32)
    group_terms = TERMS // N_MPO

    def per_sector(sector_id):
        wave_local = wave_blocks[sector_id].astype(jnp.float32)
        left_local = left_env[sector_id].astype(jnp.float32).reshape(TERMS, BLK, BLK)
        left_scaled = to_bfloat(term_gains[:, :, None, None] * left_local[:, None, :, :])
        sectioned = to_bfloat(jnp.einsum("wjlk,jkc->wjlc", left_scaled, wave_local))
        sectioned = sectioned.reshape(N_MPO, group_terms, NPB, BLK, NVEC, BLK)
        right_ids = right_sector[sector_id].astype(jnp.int32)
        right_local = right_env[right_ids].astype(jnp.float32).reshape(NPB, N_MPO, group_terms, BLK, BLK)
        group_part = to_bfloat(jnp.einsum("mtjlvr,jmtsr->mjlvs", sectioned, right_local))
        summed = jnp.sum(group_part, axis=0)
        return summed.astype(jnp.bfloat16).reshape(NPB, BLK, NVEC * BLK)

    return lax.map(per_sector, jnp.arange(NSEC, dtype=jnp.int32))
```

```python
import functools

import jax
import jax.numpy as jnp
from jax import lax
from jax.experimental import pallas as pl
from jax.experimental.pallas import tpu as pltpu
from jax.sharding import PartitionSpec as P


def pack_right(right_env, width):
    sectors, terms, _ = right_env.shape
    turned = jnp.swapaxes(right_env.reshape(sectors, terms, width, width), 2, 3)
    pairs = terms // 2
    parts = []
    if pairs:
        even = turned[:, : 2 * pairs].reshape(sectors, pairs, 2, width, width)
        even = jnp.swapaxes(even, 2, 3).reshape(sectors, pairs * width, 2 * width)
        parts.append(even)
    if terms % 2:
        odd = turned[:, -1].reshape(sectors, 2, width // 2, width)
        parts.append(jnp.swapaxes(odd, 1, 2).reshape(sectors, width // 2, 2 * width))
    return jnp.concatenate(parts, axis=1) if len(parts) > 1 else parts[0]


def block_result(wave, left_scaled, packed, terms, width):
    lanes = 2 * width
    lane = lax.broadcasted_iota(jnp.int32, (1, lanes), 1)
    low = (lane < width).astype(jnp.bfloat16)
    high = (lane >= width).astype(jnp.bfloat16)
    rolled = jnp.concatenate([packed[:, width:], packed[:, :width]], axis=1)
    groups = wave.shape[1] // lanes
    rows = jnp.concatenate([wave[:, g * lanes : (g + 1) * lanes] for g in range(groups)], axis=0)
    spread = []
    for pair in range(terms // 2):
        here, there = (m[pair * width : (pair + 1) * width] for m in (packed, rolled))
        spread.append(jnp.concatenate([here * low, there * high], axis=0))
        spread.append(jnp.concatenate([there * low, here * high], axis=0))
    if terms % 2:
        first = terms // 2 * width
        here, there = (m[first : first + width // 2] for m in (packed, rolled))
        spread.append(jnp.concatenate([here * low, there * low, there * high, here * high], axis=0))
    stacked = []
    for first in range(0, terms, 2):
        both = jnp.concatenate(spread[first : first + 2], axis=1)
        product = jnp.dot(rows, both, preferred_element_type=jnp.float32).astype(jnp.bfloat16)
        for term in range(both.shape[1] // lanes):
            cut = product[:, term * lanes : (term + 1) * lanes]
            stacked.append(
                jnp.concatenate([cut[g * width : (g + 1) * width] for g in range(groups)], axis=1)
            )
    stacked = jnp.concatenate(stacked, axis=0)
    return jnp.dot(left_scaled, stacked, preferred_element_type=jnp.float32)


def contract_kernel(terms, width, sector_ref, wave_ref, left_ref, gain_ref, right_ref, out_ref):
    classes = wave_ref.shape[1]
    row = pl.program_id(0)
    left = left_ref[0].astype(jnp.float32)
    for charge in range(classes):
        sector = sector_ref[row * classes + charge]
        left_scaled = (left * gain_ref[charge : charge + 1, :]).astype(jnp.bfloat16)
        out_ref[0, charge] = block_result(
            wave_ref[0, charge], left_scaled, right_ref[sector], terms, width
        ).astype(out_ref.dtype)


def per_device(wave_blocks, left_env, right_env, mpo_coef, mpo_mask, right_sector):
    sec_local, classes, width, columns = wave_blocks.shape
    terms = left_env.shape[1]
    bond_index = lax.axis_index("bond")
    gains = jnp.repeat((mpo_coef * mpo_mask.astype(jnp.float32)).T, width, axis=1)
    packed = pack_right(right_env, width)
    gathered = lax.all_gather(packed, "bond", axis=0, tiled=True)
    left_rows = jnp.swapaxes(left_env.reshape(sec_local, terms, width, width), 1, 2)
    left_rows = left_rows.reshape(sec_local, width, terms * width)
    sectors = lax.dynamic_slice_in_dim(right_sector, bond_index * sec_local, sec_local, 0)
    partial = pl.pallas_call(
        functools.partial(contract_kernel, terms, width),
        out_shape=jax.ShapeDtypeStruct(wave_blocks.shape, jnp.bfloat16),
        grid_spec=pltpu.PrefetchScalarGridSpec(
            num_scalar_prefetch=1,
            grid=(sec_local,),
            in_specs=[
                pl.BlockSpec((1, classes, width, columns), lambda i, s: (i, 0, 0, 0)),
                pl.BlockSpec((1, width, terms * width), lambda i, s: (i, 0, 0)),
                pl.BlockSpec(gains.shape, lambda i, s: (0, 0)),
                pl.BlockSpec(gathered.shape, lambda i, s: (0, 0, 0)),
            ],
            out_specs=pl.BlockSpec((1, classes, width, columns), lambda i, s: (i, 0, 0, 0)),
        ),
        compiler_params=pltpu.CompilerParams(vmem_limit_bytes=48 << 20),
    )(sectors.reshape(-1), wave_blocks, left_rows, gains, gathered)
    return lax.psum(partial, "mpo")


def solution(mesh):
    return jax.shard_map(
        per_device,
        mesh=mesh,
        in_specs=(
            P("bond", None, None, None),
            P("bond", "mpo", None),
            P("bond", "mpo", None),
            P("mpo", None),
            P("mpo", None),
            P(),
        ),
        out_specs=P("bond", None, None, None),
        check_vma=False,
    )
```

```python
import functools

import jax
import jax.numpy as jnp
from jax import lax
from jax.experimental import pallas as pl
from jax.experimental.pallas import tpu as pltpu
from jax.sharding import PartitionSpec as P


def pack_right(right_env, width):
    sectors, terms, _ = right_env.shape
    turned = jnp.swapaxes(right_env.reshape(sectors, terms, width, width), 2, 3)
    pairs = terms // 2
    parts = []
    if pairs:
        even = turned[:, : 2 * pairs].reshape(sectors, pairs, 2, width, width)
        even = jnp.swapaxes(even, 2, 3).reshape(sectors, pairs * width, 2 * width)
        parts.append(even)
    if terms % 2:
        odd = turned[:, -1].reshape(sectors, 2, width // 2, width)
        parts.append(jnp.swapaxes(odd, 1, 2).reshape(sectors, width // 2, 2 * width))
    return jnp.concatenate(parts, axis=1) if len(parts) > 1 else parts[0]


def block_result(wave, left_scaled, packed, terms, width):
    lanes = 2 * width
    lane = lax.broadcasted_iota(jnp.int32, (1, lanes), 1)
    low = (lane < width).astype(jnp.bfloat16)
    high = (lane >= width).astype(jnp.bfloat16)
    rolled = jnp.concatenate([packed[:, width:], packed[:, :width]], axis=1)
    groups = wave.shape[1] // lanes
    rows = jnp.concatenate([wave[:, g * lanes : (g + 1) * lanes] for g in range(groups)], axis=0)
    spread = []
    for pair in range(terms // 2):
        here, there = (m[pair * width : (pair + 1) * width] for m in (packed, rolled))
        spread.append(jnp.concatenate([here * low, there * high], axis=0))
        spread.append(jnp.concatenate([there * low, here * high], axis=0))
    if terms % 2:
        first = terms // 2 * width
        here, there = (m[first : first + width // 2] for m in (packed, rolled))
        spread.append(jnp.concatenate([here * low, there * low, there * high, here * high], axis=0))
    stacked = []
    for first in range(0, terms, 2):
        both = jnp.concatenate(spread[first : first + 2], axis=1)
        product = jnp.dot(rows, both, preferred_element_type=jnp.float32).astype(jnp.bfloat16)
        for term in range(both.shape[1] // lanes):
            cut = product[:, term * lanes : (term + 1) * lanes]
            stacked.append(
                jnp.concatenate([cut[g * width : (g + 1) * width] for g in range(groups)], axis=1)
            )
    stacked = jnp.concatenate(stacked, axis=0)
    return jnp.dot(left_scaled, stacked, preferred_element_type=jnp.float32)


MESH = pl.DeviceIdType.MESH
LAG = 2


def contract_kernel(
    terms, width, sector_ref, wave_ref, left_ref, gain_ref, right_ref, out_ref,
    mine, theirs, pair_in, pair_sum, far_in, sent, got,
):
    sectors, classes = wave_ref.shape[:2]
    steps = sectors // 2
    place = lax.axis_index("mpo")
    side = lax.rem(place, 2)
    pair = place + 1 - 2 * side
    far = lax.rem(place + 2, 4)

    barrier = pltpu.get_barrier_semaphore()
    for other in (pair, far):
        pl.semaphore_signal(barrier, inc=1, device_id={"mpo": other}, device_id_type=MESH)
    pl.semaphore_wait(barrier, 2)

    def send(kind, step, source, target, other):
        return pltpu.make_async_remote_copy(
            src_ref=source,
            dst_ref=target,
            send_sem=sent.at[kind, step],
            recv_sem=got.at[kind, step],
            device_id={"mpo": other},
            device_id_type=MESH,
        )

    def to_pair(step):
        return send(0, step, theirs.at[step], pair_in.at[step], pair)

    def to_far(step):
        return send(1, step, pair_sum.at[step], far_in.at[step], far)

    def total_copy(step, row):
        return send(2, step, out_ref.at[row], out_ref.at[row], pair)

    def contract(row, store):
        left = left_ref[row].astype(jnp.float32)
        unroll = 4 if classes % 4 == 0 else 1

        @pl.loop(0, classes // unroll)
        def _(outer):
            for inner in range(unroll):
                charge = outer * unroll + inner
                sector = sector_ref[row * classes + charge]
                left_scaled = (left * gain_ref[charge]).astype(jnp.bfloat16)
                store(
                    charge,
                    block_result(wave_ref[row, charge], left_scaled, right_ref[sector], terms, width),
                )

    def finish(step):
        to_far(step).wait_recv()
        row = 2 * step + side

        @pl.loop(0, classes)
        def _(charge):
            total = pair_sum[step, charge].astype(jnp.float32) + far_in[step, charge].astype(jnp.float32)
            out_ref[row, charge] = total.astype(out_ref.dtype)

        total_copy(step, row).start()

    @pl.loop(0, steps)
    def _(step):
        def store_theirs(charge, value):
            theirs[step, charge] = value.astype(jnp.bfloat16)

        def store_mine(charge, value):
            mine[charge] = value

        contract(2 * step + 1 - side, store_theirs)
        to_pair(step).start()
        contract(2 * step + side, store_mine)
        to_pair(step).wait_recv()

        @pl.loop(0, classes)
        def _(charge):
            both = mine[charge] + pair_in[step, charge].astype(jnp.float32)
            pair_sum[step, charge] = both.astype(jnp.bfloat16)

        to_far(step).start()

        @pl.when(step >= LAG)
        def _():
            finish(step - LAG)

    @pl.loop(max(0, steps - LAG), steps)
    def _(step):
        finish(step)

    @pl.loop(0, steps)
    def _(step):
        to_pair(step).wait_send()
        to_far(step).wait_send()
        total_copy(step, 2 * step + side).wait_send()
        total_copy(step, 2 * step + 1 - side).wait_recv()


def per_device(wave_blocks, left_env, right_env, mpo_coef, mpo_mask, right_sector):
    sec_local, classes, width, columns = wave_blocks.shape
    terms = left_env.shape[1]
    bond_index = lax.axis_index("bond")
    gains = jnp.repeat((mpo_coef * mpo_mask.astype(jnp.float32)).T, width, axis=1)
    packed = pack_right(right_env, width)
    gathered = lax.all_gather(packed, "bond", axis=0, tiled=True)
    left_rows = jnp.swapaxes(left_env.reshape(sec_local, terms, width, width), 1, 2)
    left_rows = left_rows.reshape(sec_local, width, terms * width)
    sectors = lax.dynamic_slice_in_dim(right_sector, bond_index * sec_local, sec_local, 0)
    steps = sec_local // 2
    slots = pltpu.VMEM((steps, classes, width, columns), jnp.bfloat16)
    vmem = pl.BlockSpec(memory_space=pltpu.VMEM)
    return pl.pallas_call(
        functools.partial(contract_kernel, terms, width),
        out_shape=jax.ShapeDtypeStruct(wave_blocks.shape, jnp.bfloat16),
        in_specs=[pl.BlockSpec(memory_space=pltpu.SMEM), vmem, vmem, vmem, vmem],
        out_specs=vmem,
        scratch_shapes=[
            pltpu.VMEM((classes, width, columns), jnp.float32),
            slots,
            slots,
            slots,
            slots,
            pltpu.SemaphoreType.DMA((3, steps)),
            pltpu.SemaphoreType.DMA((3, steps)),
        ],
        compiler_params=pltpu.CompilerParams(
            collective_id=0, has_side_effects=True, vmem_limit_bytes=56 << 20
        ),
    )(sectors.reshape(-1), wave_blocks, left_rows, gains[:, None, :], gathered)


def solution(mesh):
    return jax.shard_map(
        per_device,
        mesh=mesh,
        in_specs=(
            P("bond", None, None, None),
            P("bond", "mpo", None),
            P("bond", "mpo", None),
            P("mpo", None),
            P("mpo", None),
            P(),
        ),
        out_specs=P("bond", None, None, None),
        check_vma=False,
    )
```

```python
import functools

import jax
import jax.numpy as jnp
from jax import lax
from jax.experimental import pallas as pl
from jax.experimental.pallas import tpu as pltpu
from jax.sharding import PartitionSpec as P


def pack_right(right_env, width):
    sectors, terms, _ = right_env.shape
    squares = right_env.reshape(sectors, terms, width, width)
    pairs = terms // 2
    parts = []
    if pairs:
        even = squares[:, : 2 * pairs].reshape(sectors, pairs, 2, width, width)
        even = jnp.swapaxes(even, 2, 3).reshape(sectors, pairs * width, 2 * width)
        parts.append(even)
    if terms % 2:
        odd = squares[:, -1].reshape(sectors, 2, width // 2, width)
        parts.append(jnp.swapaxes(odd, 1, 2).reshape(sectors, width // 2, 2 * width))
    return jnp.concatenate(parts, axis=1) if len(parts) > 1 else parts[0]


def block_result(wave, left_scaled, packed, terms, width):
    lanes = 2 * width
    lane = lax.broadcasted_iota(jnp.int32, (1, lanes), 1)
    low = (lane < width).astype(jnp.bfloat16)
    high = (lane >= width).astype(jnp.bfloat16)
    rolled = jnp.concatenate([packed[:, width:], packed[:, :width]], axis=1)
    groups = wave.shape[1] // lanes
    rows = jnp.concatenate([wave[:, g * lanes : (g + 1) * lanes] for g in range(groups)], axis=0)
    spread = []
    for pair in range(terms // 2):
        here, there = (m[pair * width : (pair + 1) * width] for m in (packed, rolled))
        spread.append(jnp.concatenate([here * low, there * high], axis=0))
        spread.append(jnp.concatenate([there * low, here * high], axis=0))
    if terms % 2:
        first = terms // 2 * width
        here, there = (m[first : first + width // 2] for m in (packed, rolled))
        spread.append(jnp.concatenate([here * low, there * low, there * high, here * high], axis=0))
    stacked = []
    for first in range(0, terms, 2):
        both = jnp.concatenate(spread[first : first + 2], axis=0)
        product = lax.dot_general(
            rows, both, (((1,), (1,)), ((), ())), preferred_element_type=jnp.float32
        ).astype(jnp.bfloat16)
        for term in range(both.shape[0] // lanes):
            cut = product[:, term * lanes : (term + 1) * lanes]
            stacked.append(
                jnp.concatenate([cut[g * width : (g + 1) * width] for g in range(groups)], axis=1)
            )
    stacked = jnp.concatenate(stacked, axis=0)
    return jnp.dot(left_scaled, stacked, preferred_element_type=jnp.float32)


MESH = pl.DeviceIdType.MESH
LAG = 2


def contract_kernel(
    terms, width, sector_ref, wave_ref, left_ref, gain_ref, right_ref, out_ref,
    mine, theirs, pair_in, pair_sum, far_in, sent, got,
):
    sectors, classes = wave_ref.shape[:2]
    steps = sectors // 2
    place = lax.axis_index("mpo")
    side = lax.rem(place, 2)
    pair = place + 1 - 2 * side
    far = lax.rem(place + 2, 4)

    barrier = pltpu.get_barrier_semaphore()
    for other in (pair, far):
        pl.semaphore_signal(barrier, inc=1, device_id={"mpo": other}, device_id_type=MESH)
    pl.semaphore_wait(barrier, 2)

    def send(kind, step, source, target, other):
        return pltpu.make_async_remote_copy(
            src_ref=source,
            dst_ref=target,
            send_sem=sent.at[kind, step],
            recv_sem=got.at[kind, step],
            device_id={"mpo": other},
            device_id_type=MESH,
        )

    def to_pair(step):
        return send(0, step, theirs.at[step], pair_in.at[step], pair)

    def to_far(step):
        return send(1, step, pair_sum.at[step], far_in.at[step], far)

    def total_copy(step, row):
        return send(2, step, out_ref.at[row], out_ref.at[row], pair)

    def contract(row, store):
        left = left_ref[row].astype(jnp.float32)
        unroll = 4 if classes % 4 == 0 else 1

        @pl.loop(0, classes // unroll)
        def _(outer):
            for inner in range(unroll):
                charge = outer * unroll + inner
                sector = sector_ref[row * classes + charge]
                left_scaled = (left * gain_ref[charge]).astype(jnp.bfloat16)
                store(
                    charge,
                    block_result(wave_ref[row, charge], left_scaled, right_ref[sector], terms, width),
                )

    def finish(step):
        to_far(step).wait_recv()
        row = 2 * step + side

        @pl.loop(0, classes)
        def _(charge):
            total = pair_sum[step, charge].astype(jnp.float32) + far_in[step, charge].astype(jnp.float32)
            out_ref[row, charge] = total.astype(out_ref.dtype)

        total_copy(step, row).start()

    @pl.loop(0, steps)
    def _(step):
        def store_theirs(charge, value):
            theirs[step, charge] = value.astype(jnp.bfloat16)

        def store_mine(charge, value):
            mine[charge] = value

        contract(2 * step + 1 - side, store_theirs)
        to_pair(step).start()
        contract(2 * step + side, store_mine)
        to_pair(step).wait_recv()

        @pl.loop(0, classes)
        def _(charge):
            both = mine[charge] + pair_in[step, charge].astype(jnp.float32)
            pair_sum[step, charge] = both.astype(jnp.bfloat16)

        to_far(step).start()

        @pl.when(step >= LAG)
        def _():
            finish(step - LAG)

    @pl.loop(max(0, steps - LAG), steps)
    def _(step):
        finish(step)

    @pl.loop(0, steps)
    def _(step):
        to_pair(step).wait_send()
        to_far(step).wait_send()
        total_copy(step, 2 * step + side).wait_send()
        total_copy(step, 2 * step + 1 - side).wait_recv()


def per_device(wave_blocks, left_env, right_env, mpo_coef, mpo_mask, right_sector):
    sec_local, classes, width, columns = wave_blocks.shape
    terms = left_env.shape[1]
    bond_index = lax.axis_index("bond")
    gains = jnp.repeat((mpo_coef * mpo_mask.astype(jnp.float32)).T, width, axis=1)
    packed = pack_right(right_env, width)
    gathered = lax.all_gather(packed, "bond", axis=0, tiled=True)
    left_rows = jnp.swapaxes(left_env.reshape(sec_local, terms, width, width), 1, 2)
    left_rows = left_rows.reshape(sec_local, width, terms * width)
    sectors = lax.dynamic_slice_in_dim(right_sector, bond_index * sec_local, sec_local, 0)
    steps = sec_local // 2
    slots = pltpu.VMEM((steps, classes, width, columns), jnp.bfloat16)
    vmem = pl.BlockSpec(memory_space=pltpu.VMEM)
    return pl.pallas_call(
        functools.partial(contract_kernel, terms, width),
        out_shape=jax.ShapeDtypeStruct(wave_blocks.shape, jnp.bfloat16),
        in_specs=[pl.BlockSpec(memory_space=pltpu.SMEM), vmem, vmem, vmem, vmem],
        out_specs=vmem,
        scratch_shapes=[
            pltpu.VMEM((classes, width, columns), jnp.float32),
            slots,
            slots,
            slots,
            slots,
            pltpu.SemaphoreType.DMA((3, steps)),
            pltpu.SemaphoreType.DMA((3, steps)),
        ],
        compiler_params=pltpu.CompilerParams(
            collective_id=0, has_side_effects=True, vmem_limit_bytes=56 << 20
        ),
    )(sectors.reshape(-1), wave_blocks, left_rows, gains[:, None, :], gathered)


def solution(mesh):
    return jax.shard_map(
        per_device,
        mesh=mesh,
        in_specs=(
            P("bond", None, None, None),
            P("bond", "mpo", None),
            P("bond", "mpo", None),
            P("mpo", None),
            P("mpo", None),
            P(),
        ),
        out_specs=P("bond", None, None, None),
        check_vma=False,
    )
```

```python
import functools

import jax
import jax.numpy as jnp
from jax import lax
from jax.experimental import pallas as pl
from jax.experimental.pallas import tpu as pltpu
from jax.sharding import PartitionSpec as P


def pack_right(right_env, width):
    sectors, terms, _ = right_env.shape
    squares = right_env.reshape(sectors, terms, width, width)
    pairs = terms // 2
    parts = []
    if pairs:
        even = squares[:, : 2 * pairs].reshape(sectors, pairs, 2, width, width)
        even = jnp.swapaxes(even, 2, 3).reshape(sectors, pairs * width, 2 * width)
        parts.append(even)
    if terms % 2:
        odd = squares[:, -1].reshape(sectors, 2, width // 2, width)
        parts.append(jnp.swapaxes(odd, 1, 2).reshape(sectors, width // 2, 2 * width))
    return jnp.concatenate(parts, axis=1) if len(parts) > 1 else parts[0]


def block_result(wave, left_scaled, packed, terms, width):
    lanes = 2 * width
    lane = lax.broadcasted_iota(jnp.int32, (1, lanes), 1)
    low = (lane < width).astype(jnp.bfloat16)
    high = (lane >= width).astype(jnp.bfloat16)
    rolled = jnp.concatenate([packed[:, width:], packed[:, :width]], axis=1)
    groups = wave.shape[1] // lanes
    rows = jnp.concatenate([wave[:, g * lanes : (g + 1) * lanes] for g in range(groups)], axis=0)
    spread = []
    for pair in range(terms // 2):
        here, there = (m[pair * width : (pair + 1) * width] for m in (packed, rolled))
        spread.append(jnp.concatenate([here * low, there * high], axis=0))
        spread.append(jnp.concatenate([there * low, here * high], axis=0))
    if terms % 2:
        first = terms // 2 * width
        here, there = (m[first : first + width // 2] for m in (packed, rolled))
        spread.append(jnp.concatenate([here * low, there * low, there * high, here * high], axis=0))
    stacked = []
    for first in range(0, terms, 2):
        both = jnp.concatenate(spread[first : first + 2], axis=0)
        product = lax.dot_general(
            rows, both, (((1,), (1,)), ((), ())), preferred_element_type=jnp.float32
        ).astype(jnp.bfloat16)
        for term in range(both.shape[0] // lanes):
            cut = product[:, term * lanes : (term + 1) * lanes]
            stacked.append(
                jnp.concatenate([cut[g * width : (g + 1) * width] for g in range(groups)], axis=1)
            )
    stacked = jnp.concatenate(stacked, axis=0)
    return jnp.dot(left_scaled, stacked, preferred_element_type=jnp.float32)


MESH = pl.DeviceIdType.MESH
LAG = 2


def contract_kernel(
    terms, width, sector_ref, wave_hbm, left_ref, gain_ref, right_ref, out_ref,
    wave_ref, mine, theirs, pair_in, pair_sum, far_in, loaded, sent, got,
):
    sectors, classes = wave_ref.shape[:2]
    steps = sectors // 2
    place = lax.axis_index("mpo")
    side = lax.rem(place, 2)
    pair = place + 1 - 2 * side
    far = lax.rem(place + 2, 4)

    def load(step):
        rows = pl.ds(2 * step, 2)
        return pltpu.make_async_copy(wave_hbm.at[rows], wave_ref.at[rows], loaded.at[step])

    @pl.loop(0, steps)
    def _(step):
        load(step).start()

    barrier = pltpu.get_barrier_semaphore()
    for other in (pair, far):
        pl.semaphore_signal(barrier, inc=1, device_id={"mpo": other}, device_id_type=MESH)
    pl.semaphore_wait(barrier, 2)

    def send(kind, step, source, target, other):
        return pltpu.make_async_remote_copy(
            src_ref=source,
            dst_ref=target,
            send_sem=sent.at[kind, step],
            recv_sem=got.at[kind, step],
            device_id={"mpo": other},
            device_id_type=MESH,
        )

    def to_pair(step):
        return send(0, step, theirs.at[step], pair_in.at[step], pair)

    def to_far(step):
        return send(1, step, pair_sum.at[step], far_in.at[step], far)

    def total_copy(step, row):
        return send(2, step, out_ref.at[row], out_ref.at[row], pair)

    def contract(row, store):
        left = left_ref[row].astype(jnp.float32)
        unroll = 4 if classes % 4 == 0 else 1

        @pl.loop(0, classes // unroll)
        def _(outer):
            for inner in range(unroll):
                charge = outer * unroll + inner
                sector = sector_ref[row * classes + charge]
                left_scaled = (left * gain_ref[charge]).astype(jnp.bfloat16)
                store(
                    charge,
                    block_result(wave_ref[row, charge], left_scaled, right_ref[sector], terms, width),
                )

    def finish(step):
        to_far(step).wait_recv()
        row = 2 * step + side

        @pl.loop(0, classes)
        def _(charge):
            total = pair_sum[step, charge].astype(jnp.float32) + far_in[step, charge].astype(jnp.float32)
            out_ref[row, charge] = total.astype(out_ref.dtype)

        total_copy(step, row).start()

    @pl.loop(0, steps)
    def _(step):
        def store_theirs(charge, value):
            theirs[step, charge] = value.astype(jnp.bfloat16)

        def store_mine(charge, value):
            mine[charge] = value

        load(step).wait()
        contract(2 * step + 1 - side, store_theirs)
        to_pair(step).start()
        contract(2 * step + side, store_mine)
        to_pair(step).wait_recv()

        @pl.loop(0, classes)
        def _(charge):
            both = mine[charge] + pair_in[step, charge].astype(jnp.float32)
            pair_sum[step, charge] = both.astype(jnp.bfloat16)

        to_far(step).start()

        @pl.when(step >= LAG)
        def _():
            finish(step - LAG)

    @pl.loop(max(0, steps - LAG), steps)
    def _(step):
        finish(step)

    @pl.loop(0, steps)
    def _(step):
        to_pair(step).wait_send()
        to_far(step).wait_send()
        total_copy(step, 2 * step + side).wait_send()
        total_copy(step, 2 * step + 1 - side).wait_recv()


def per_device(wave_blocks, left_env, right_env, mpo_coef, mpo_mask, right_sector):
    sec_local, classes, width, columns = wave_blocks.shape
    terms = left_env.shape[1]
    bond_index = lax.axis_index("bond")
    gains = jnp.repeat((mpo_coef * mpo_mask.astype(jnp.float32)).T, width, axis=1)
    packed = pack_right(right_env, width)
    gathered = lax.all_gather(packed, "bond", axis=0, tiled=True)
    left_rows = jnp.swapaxes(left_env.reshape(sec_local, terms, width, width), 1, 2)
    left_rows = left_rows.reshape(sec_local, width, terms * width)
    sectors = lax.dynamic_slice_in_dim(right_sector, bond_index * sec_local, sec_local, 0)
    steps = sec_local // 2
    slots = pltpu.VMEM((steps, classes, width, columns), jnp.bfloat16)
    vmem = pl.BlockSpec(memory_space=pltpu.VMEM)
    return pl.pallas_call(
        functools.partial(contract_kernel, terms, width),
        out_shape=jax.ShapeDtypeStruct(wave_blocks.shape, jnp.bfloat16),
        in_specs=[pl.BlockSpec(memory_space=pltpu.SMEM), pl.BlockSpec(memory_space=pl.ANY), vmem, vmem, vmem],
        out_specs=vmem,
        scratch_shapes=[
            pltpu.VMEM(wave_blocks.shape, jnp.bfloat16),
            pltpu.VMEM((classes, width, columns), jnp.float32),
            slots,
            slots,
            slots,
            slots,
            pltpu.SemaphoreType.DMA((steps,)),
            pltpu.SemaphoreType.DMA((3, steps)),
            pltpu.SemaphoreType.DMA((3, steps)),
        ],
        compiler_params=pltpu.CompilerParams(
            collective_id=0, has_side_effects=True, vmem_limit_bytes=56 << 20
        ),
    )(sectors.reshape(-1), wave_blocks, left_rows, gains[:, None, :], gathered)


def solution(mesh):
    return jax.shard_map(
        per_device,
        mesh=mesh,
        in_specs=(
            P("bond", None, None, None),
            P("bond", "mpo", None),
            P("bond", "mpo", None),
            P("mpo", None),
            P("mpo", None),
            P(),
        ),
        out_specs=P("bond", None, None, None),
        check_vma=False,
    )
```
